512 devices in a mesh: gx: 8 (over y, core), gy: 8 (over z_hi, x), gz: 8 (over z_lo).
Axes of the slice: x: 4, y: 4, z: 16 (z_hi: 2, z_lo: 8; z = z_hi * 8 + z_lo), core: 2. Of those that a mesh axis runs over, the one named last changes fastest.
Arguments:
- activations: bfloat16 [8, 128, 6144], P('gy', 'gx', 'gz'), may hold values from -6 to 6
- cotangent: bfloat16 [8, 128, 6144], P('gy', 'gx', 'gz'), may hold values from -6 to 6
- probe: int32 [8, 128, 6144], P('gy', None, 'gz'), may hold values from 0 to 1
- w_in: bfloat16 [6144, 24576], P('gz', ('gx', 'gy')), may hold values from -0.078125 to 0.078125
- w_out: bfloat16 [24576, 6144], P(('gx', 'gy'), 'gz'), may hold values from -0.0390625 to 0.0390625
Outputs:
- gradient: bfloat16 [8, 128, 6144], P('gy', 'gx', 'gz')
- curvature_product: bfloat16 [8, 128, 6144], P('gy', 'gx', 'gz')
The draws below stay inside these ranges and needn't reach their ends.
All inputs are finite; a program needn't handle non-finite values.
Results may differ from the reference program's by a relative error of at most 0.035.
Values may be sent and summed in bfloat16 or wider, within the bound.
A program may use at most 64 MiB of HBM per device.

```python
import jax
import jax.numpy as jnp

D = 6144
FF = 24576
ROWS = 128
GROUPS = 8
N_GX = 8
N_GZ = 8


def plant(result, rng, low, high):
    index_at = [jax.random.randint(jax.random.fold_in(rng, axis), (), 0, length) for axis, length in enumerate(result.shape)]
    longest = result.shape.index(max(result.shape))
    next_to = index_at[:longest] + [(index_at[longest] + 1) % result.shape[longest]] + index_at[longest + 1:]
    return result.at[tuple(index_at)].set(low).at[tuple(next_to)].set(high)


def block_scale(stream_key, dims, shards, smallest, largest):
    loudness = 1.0
    for dim, parts in shards:
        heights = jax.random.uniform(jax.random.fold_in(jax.random.fold_in(stream_key, 6), dim), (parts,), jnp.float32, smallest / len(shards), largest / len(shards))
        loudness = loudness * jnp.repeat(jnp.exp(heights), dims[dim] // parts).reshape((-1,) + (1,) * (len(dims) - 1 - dim))
    return loudness


def noise(rng, extent, deviation, bound, cuts=(), kind=jnp.bfloat16):
    array = deviation * jax.random.normal(rng, extent, jnp.float32)
    if cuts:
        array = array * block_scale(rng, extent, cuts, -0.22, 0.18)
    return jnp.clip(array, -bound, bound).astype(kind)


def setup_inputs(seed: int = 0) -> dict:
    key_list = jax.random.split(jax.random.key(seed), 6)
    activations = noise(key_list[0], (GROUPS, ROWS, D), 1.0, 6.0, ((0, 8), (1, 8), (2, 8)))
    cotangent = noise(key_list[1], (GROUPS, ROWS, D), 1.0, 6.0, ((0, 8), (1, 8), (2, 8)))
    probe = plant(jax.random.randint(key_list[2], (GROUPS, ROWS, D), 0, 2), jax.random.fold_in(key_list[2], 1), 0, 1).astype(jnp.int32)
    w_in = noise(key_list[3], (D, FF), D ** -0.5, 0.078125, ((0, 8), (1, 64)))
    w_out = noise(key_list[4], (FF, D), FF ** -0.5, 0.0390625, ((0, 64), (1, 8)))
    return {"activations": activations, "cotangent": cotangent, "probe": probe, "w_in": w_in, "w_out": w_out}


def density(value):
    return jnp.exp(-0.5 * value * value) * 0.3989422804014327


def normal_cdf(value):
    return 0.5 * (1.0 + jax.scipy.special.erf(value * 0.7071067811865476))


def feature_sum(left, right_rows):
    width_block = D // N_GZ
    total = jnp.zeros((left.shape[0], right_rows.shape[1]), jnp.float32)
    for index in range(N_GZ):
        lo = index * width_block
        part = jnp.dot(left[:, lo:lo + width_block], right_rows[lo:lo + width_block, :], preferred_element_type=jnp.float32)
        total = total + part.astype(jnp.bfloat16).astype(jnp.float32)
    return total


def hidden_sum(left, weight):
    width_block = FF // N_GX
    total = jnp.zeros((left.shape[0], D), jnp.float32)
    for index in range(N_GX):
        lo = index * width_block
        part = jnp.dot(left[:, lo:lo + width_block], weight[:, lo:lo + width_block].T, preferred_element_type=jnp.float32)
        total = total + part.astype(jnp.bfloat16).astype(jnp.float32)
    return total


def reference(activations, cotangent, probe, w_in, w_out):
    tokens = activations.reshape(GROUPS * ROWS, D)
    cot_rows = cotangent.reshape(GROUPS * ROWS, D)
    direction = (2 * probe - 1).astype(jnp.bfloat16).reshape(GROUPS * ROWS, D)
    hidden = feature_sum(tokens, w_in)
    tangent = feature_sum(direction, w_in)
    upstream = feature_sum(cot_rows, w_out.T)
    dens = density(hidden)
    slope = ((normal_cdf(hidden) + hidden * dens) * upstream).astype(jnp.bfloat16)
    curve = (dens * (2.0 - hidden * hidden) * tangent * upstream).astype(jnp.bfloat16)
    gradient = hidden_sum(slope, w_in).astype(jnp.bfloat16).reshape(GROUPS, ROWS, D)
    curvature_product = hidden_sum(curve, w_in).astype(jnp.bfloat16).reshape(GROUPS, ROWS, D)
    return gradient, curvature_product
```

```python
import functools

import jax
import jax.numpy as jnp
from jax import lax
from jax.experimental import pallas as pl
from jax.experimental.pallas import tpu as pltpu
from jax.sharding import PartitionSpec as P

MESH = pl.DeviceIdType.MESH
BF16, F32 = jnp.bfloat16, jnp.float32

PAIRS = 32
LAG = 2
FWD = 2
BWD = 2
AHEAD = 3
CORE_LAG = 2
HI_LAG = 4


def other_half(p):
    return lax.rem(lax.div(p + 8, 16), 2)


def kernel(act, cot, probe, w_in, w_out, grad, curv,
           A, PART, CI, CM, CS, SB, OP, OCS, OCR, OXS, OXR, ZS, ZR, bits, w_in_t, w_out_t,
           bits_sem, hi_s, hi_r, axy_s, axy_r, ac_s, ac_r, c_s, ci_r, cm_r, so_s, si_s, s_r,
           oc_s, oc_r, ox_s, ox_r, z_s, z_r):
    gx, gy, z = lax.axis_index("gx"), lax.axis_index("gy"), lax.axis_index("gz")
    y, core = lax.div(gx, 2), lax.rem(gx, 2)
    hi, x = lax.div(gy, 4), lax.rem(gy, 4)
    left = z < 4
    edge = lax.select(left, z, 7 - z)
    z_in = lax.select(left, z + 1, z - 1)
    z_out = lax.select(left, z - 1, z + 1)

    def at(dx, dy):
        return (lax.rem(y + dy, 4) * 2 + core, hi * 4 + lax.rem(x + dx, 4), z)

    partner = (y * 2 + 1 - core, gy, z)
    across = (gx, (1 - hi) * 4 + x, z)
    inner, outer = (gx, gy, z_in), (gx, gy, z_out)

    def send(src, dst, s, r, device):
        return pltpu.make_async_remote_copy(
            src_ref=src, dst_ref=dst, send_sem=s, recv_sem=r, device_id=device, device_id_type=MESH)

    def hi_copy():
        return send(A.at[0, 0], A.at[16, 0], hi_s, hi_r, across)

    def axy_copy(p):
        q = lax.rem(p, 16)
        return send(A.at[16 * other_half(p), 0], A.at[p, 0], axy_s.at[p], axy_r.at[p],
                    at(4 - lax.rem(q, 4), 4 - lax.div(q, 4)))

    def ac_copy(p):
        return send(A.at[p, 0], A.at[p, 1], ac_s.at[p], ac_r.at[p], partner)

    def ci_copy(p, c):
        return send(CS.at[p, c], CI.at[p, c], c_s.at[p, c], ci_r.at[p, c], inner)

    def cm_copy(p, c):
        return send(CS.at[p, c], CM.at[p], c_s.at[p, c], cm_r.at[p], inner)

    def so_copy(p, c):
        return send(SB.at[p, c], SB.at[p, c], so_s.at[p, c], s_r.at[p, c], outer)

    def si_copy(p, c):
        return send(SB.at[p, c], SB.at[p, c], si_s.at[p], s_r.at[p, c], inner)

    def oc_copy(p):
        return send(OCS.at[p], OCR.at[p], oc_s.at[p], oc_r.at[p], partner)

    def ox_copy(p):
        q = lax.rem(p, 16)
        return send(OXS.at[p], OXR.at[p], ox_s.at[p], ox_r.at[p], at(lax.rem(q, 4), lax.div(q, 4)))

    def z_copy():
        return send(ZS, ZR, z_s, z_r, across)

    bits_copy = pltpu.make_async_copy(probe.at[pl.ds(pl.multiple_of(gx * 16, 16), 16)], bits, bits_sem)
    bits_copy.start()

    barrier = pltpu.get_barrier_semaphore()

    def greet(device):
        pl.semaphore_signal(barrier, inc=1, device_id=device, device_id_type=MESH)

    for q in range(1, 16):
        greet(at(q % 4, q // 4))
    greet(partner)
    greet(across)
    greet(inner)

    @pl.when(edge > 0)
    def _():
        greet(outer)

    A[0, 0, 0:16, :] = act[...]
    A[0, 0, 32:48, :] = cot[...]
    bits_copy.wait()
    A[0, 0, 16:32, :] = (2 * bits[...] - 1).astype(F32).astype(BF16)
    pl.semaphore_wait(barrier, 18 + lax.select(edge > 0, 1, 0))

    ac_copy(0).start()
    hi_copy().start()
    lax.fori_loop(1, 8, lambda p, t: (axy_copy(p).start(), t)[1], 0)
    w_in_t[...] = w_in[...].T
    w_out_t[...] = w_out[...].T

    def collect(p):
        axy_copy(p).wait_recv()
        ac_copy(p).start()

    lax.fori_loop(1, AHEAD, lambda p, t: (collect(p), t)[1], 0)

    def forward(p):
        def arrived(i, t):
            ac_copy(p + i).wait_recv()
            return t

        lax.fori_loop(0, FWD, arrived, 0)
        rows = pl.ds(p, FWD)
        left_rows = A[rows, :, 0:32, :].reshape(FWD * 64, 768)
        PART[rows, :, 0:32, :] = jnp.dot(
            left_rows, w_in[...], preferred_element_type=F32).reshape(FWD, 2, 32, 384)
        cot_rows = A[rows, :, 32:48, :].reshape(FWD * 32, 768)
        PART[rows, :, 32:48, :] = jnp.dot(
            cot_rows, w_out_t[...], preferred_element_type=F32).reshape(FWD, 2, 16, 384)

    def chain(p, c):
        @pl.when(edge == 0)
        def _():
            CS[p, c] = PART[p, c].astype(BF16)

        @pl.when(edge > 0)
        def _():
            ci_copy(p, c).wait_recv()
            CS[p, c] = (PART[p, c] + CI[p, c].astype(F32)).astype(BF16)

        @pl.when(edge < 3)
        def _():
            ci_copy(p, c).start()

        @pl.when(edge == 3)
        def _():
            cm_copy(p, c).start()

    def finish(p, c):
        ci_copy(p, c).wait_recv()
        cm_copy(p, c).wait_recv()
        total = PART[p, c] + CI[p, c].astype(F32) + CM[p].astype(F32)
        hidden, tangent, upstream = total[0:16], total[16:32], total[32:48]
        dens = jnp.exp(-0.5 * hidden * hidden) * 0.3989422804014327
        cdf = 0.5 * (1.0 + lax.erf(hidden * 0.7071067811865476))
        SB[p, c, 0:16, :] = ((cdf + hidden * dens) * upstream).astype(BF16)
        SB[p, c, 16:32, :] = (dens * (2.0 - hidden * hidden) * tangent * upstream).astype(BF16)
        so_copy(p, c).start()
        si_copy(p, c).start()

    def spread(p, c):
        so_copy(p, c).wait_recv()

        @pl.when(edge > 0)
        def _():
            so_copy(p, c).start()

    def backward(p):
        rows = pl.ds(p, BWD)
        out = jnp.dot(SB[rows].reshape(BWD * 64, 384), w_in_t[...], preferred_element_type=F32)
        out = out.reshape(BWD, 2, 32, 768)
        OP[rows] = out[:, 0]
        OCS[rows] = out[:, 1].astype(BF16)
        lax.fori_loop(0, BWD, lambda i, t: (oc_copy(p + i).start(), t)[1], 0)

    def join(p):
        oc_copy(p).wait_recv()
        total = OP[p] + OCR[p].astype(F32)

        @pl.when(lax.rem(p, 16) == 0)
        def _():
            OP[p] = total

        @pl.when(lax.rem(p, 16) != 0)
        def _():
            OXS[p] = total.astype(BF16)
            ox_copy(p).start()

    def gather_sum(own, first, last):
        def add(p, total):
            ox_copy(p).wait_recv()
            return total + OXR[p].astype(F32)

        total = OP[own]
        for lo, hi_ in first, last:
            total = lax.fori_loop(lo, hi_, add, total)
        return total

    def within(p):
        return jnp.logical_and(p >= 0, p < PAIRS)

    def step(s, t):
        def pass_on(p):
            @pl.when(jnp.logical_and(jnp.logical_and(p >= 8, p < PAIRS), p != 16))
            def _():
                @pl.when(p == 8)
                def _():
                    hi_copy().wait_recv()
                    ac_copy(16).start()

                axy_copy(p).start()

        pass_on(2 * s)
        pass_on(2 * s + 1)

        @pl.when(jnp.logical_and(s + AHEAD < PAIRS, s + AHEAD != 16))
        def _():
            collect(s + AHEAD)

        pc = s - LAG * edge

        @pl.when(jnp.logical_and(within(pc), lax.rem(pc + 64, FWD) == 0))
        def _():
            forward(pc)

        for c in range(2):
            @pl.when(jnp.logical_and(within(pc), z != 3 + c))
            def _():
                chain(pc, c)

            pf = s - LAG * 4

            @pl.when(jnp.logical_and(within(pf), z == 3 + c))
            def _():
                finish(pf, c)

            away = lax.select(z < 3 + c, 3 + c - z, z - 3 - c)
            ps = s - LAG * (4 + away)

            @pl.when(jnp.logical_and(within(ps), z != 3 + c))
            def _():
                spread(ps, c)

        pb = s - LAG * (8 - edge)

        @pl.when(jnp.logical_and(within(pb), lax.rem(pb + 64, BWD) == BWD - 1))
        def _():
            backward(pb - BWD + 1)

        pj = pb - CORE_LAG

        @pl.when(within(pj))
        def _():
            join(pj)

        @pl.when(pj == 23 + HI_LAG)
        def _():
            ZS[...] = gather_sum(16, (8, 16), (17, 24)).astype(BF16)
            z_copy().start()

        return t

    lax.fori_loop(0, PAIRS + LAG * 8 + CORE_LAG, step, 0)

    total = gather_sum(0, (1, 8), (24, 32))
    z_copy().wait_recv()
    total = total + ZR[...].astype(F32)
    grad[...] = total[0:16].astype(BF16)
    curv[...] = total[16:32].astype(BF16)

    hi_copy().wait_send()
    z_copy().wait_send()

    def sent(p, t):
        ac_copy(p).wait_send()
        oc_copy(p).wait_send()

        @pl.when(lax.rem(p, 16) != 0)
        def _():
            axy_copy(p).wait_send()
            ox_copy(p).wait_send()

        for c in range(2):
            @pl.when(z != 3 + c)
            def _():
                ci_copy(p, c).wait_send()

            @pl.when(z == 3 + c)
            def _():
                si_copy(p, c).wait_send()

            @pl.when(edge > 0)
            def _():
                so_copy(p, c).wait_send()
        return t

    lax.fori_loop(0, PAIRS, sent, 0)


def per_device(activations, cotangent, probe, w_in, w_out):
    n = PAIRS
    dma = pltpu.SemaphoreType.DMA
    vmem = pl.BlockSpec(memory_space=pltpu.VMEM)
    gradient, curvature = pl.pallas_call(
        kernel,
        out_shape=(jax.ShapeDtypeStruct((16, 768), BF16),) * 2,
        in_specs=[vmem, vmem, pl.BlockSpec(memory_space=pl.ANY), vmem, vmem],
        out_specs=(vmem, vmem),
        scratch_shapes=[
            pltpu.VMEM((n, 2, 48, 768), BF16),
            pltpu.VMEM((n, 2, 48, 384), F32),
            pltpu.VMEM((n, 2, 48, 384), BF16),
            pltpu.VMEM((n, 48, 384), BF16),
            pltpu.VMEM((n, 2, 48, 384), BF16),
            pltpu.VMEM((n, 2, 32, 384), BF16),
            pltpu.VMEM((n, 32, 768), F32),
            pltpu.VMEM((n, 32, 768), BF16),
            pltpu.VMEM((n, 32, 768), BF16),
            pltpu.VMEM((n, 32, 768), BF16),
            pltpu.VMEM((n, 32, 768), BF16),
            pltpu.VMEM((32, 768), BF16),
            pltpu.VMEM((32, 768), BF16),
            pltpu.VMEM((16, 768), jnp.int32),
            pltpu.VMEM((384, 768), BF16),
            pltpu.VMEM((768, 384), BF16),
            dma, dma, dma,
            dma((n,)), dma((n,)), dma((n,)), dma((n,)),
            dma((n, 2)), dma((n, 2)), dma((n,)),
            dma((n, 2)), dma((n,)), dma((n, 2)),
            dma((n,)), dma((n,)), dma((n,)), dma((n,)),
            dma, dma,
        ],
        compiler_params=pltpu.CompilerParams(
            collective_id=0, has_side_effects=True, vmem_limit_bytes=60 * 1024 * 1024),
        cost_estimate=pl.CostEstimate(flops=3_020_000_000, bytes_accessed=3_000_000, transcendentals=400_000),
    )(activations[0], cotangent[0], probe[0], w_in, w_out)
    return gradient[None], curvature[None]


def solution(mesh):
    placed = (
        P("gy", "gx", "gz"),
        P("gy", "gx", "gz"),
        P("gy", None, "gz"),
        P("gz", ("gx", "gy")),
        P(("gx", "gy"), "gz"),
    )
    return jax.shard_map(
        per_device,
        mesh=mesh,
        in_specs=placed,
        out_specs=(P("gy", "gx", "gz"), P("gy", "gx", "gz")),
        check_vma=False,
    )
```

```python
import functools

import jax
import jax.numpy as jnp
from jax import lax
from jax.experimental import pallas as pl
from jax.experimental.pallas import tpu as pltpu
from jax.sharding import PartitionSpec as P

MESH = pl.DeviceIdType.MESH
BF16, F32 = jnp.bfloat16, jnp.float32

PAIRS = 32
CHUNKS = 2 * PAIRS
FIRST = 10
LAG = 3
EARLY = 6
AHEAD = 3
CORE_LAG = 2
HI_LAG = 2


def other_half(p):
    return lax.rem(lax.div(p + 16 - FIRST, 16), 2)


def kernel(act, cot, probe, w_in_hbm, w_out_hbm, grad, curv,
           A, PART, CI, CM, CS, SB, OP, OCS, OCR, OXS, OXR, ZS, ZR, bits, w_in, w_out, w_in_t, w_out_t,
           load_sem, hi_s, hi_r, axy_s, axy_r, ac_s, ac_r, c_s, ci_r, cm_r, so_s, si_s, s_r,
           oc_s, oc_r, ox_s, ox_r, z_s, z_r):
    gx, gy, z = lax.axis_index("gx"), lax.axis_index("gy"), lax.axis_index("gz")
    y, core = lax.div(gx, 2), lax.rem(gx, 2)
    hi, x = lax.div(gy, 4), lax.rem(gy, 4)
    left = z < 4
    edge = lax.select(left, z, 7 - z)
    z_in = lax.select(left, z + 1, z - 1)
    z_out = lax.select(left, z - 1, z + 1)

    def at(dx, dy):
        return (lax.rem(y + dy, 4) * 2 + core, hi * 4 + lax.rem(x + dx, 4), z)

    partner = (y * 2 + 1 - core, gy, z)
    across = (gx, (1 - hi) * 4 + x, z)
    inner, outer = (gx, gy, z_in), (gx, gy, z_out)

    def send(src, dst, s, r, device):
        return pltpu.make_async_remote_copy(
            src_ref=src, dst_ref=dst, send_sem=s, recv_sem=r, device_id=device, device_id_type=MESH)

    def hi_copy():
        return send(A.at[0], A.at[32], hi_s, hi_r, across)

    def axy_copy(p):
        q = lax.rem(p, 16)
        return send(A.at[32 * other_half(p)], A.at[2 * p], axy_s, axy_r.at[p],
                    at(4 - lax.rem(q, 4), 4 - lax.rem(3 * q + lax.div(q, 4), 4)))

    def ac_copy(p):
        return send(A.at[2 * p], A.at[2 * p + 1], ac_s, ac_r.at[p], partner)

    def ci_copy(k):
        return send(CS.at[k], CI.at[k], c_s, ci_r.at[k], inner)

    def cm_copy(k):
        p = lax.div(k, 2)
        return send(CS.at[k], CM.at[p], c_s, cm_r.at[p], inner)

    def so_copy(k):
        return send(SB.at[k], SB.at[k], so_s, s_r.at[k], outer)

    def si_copy(k):
        return send(SB.at[k], SB.at[k], si_s, s_r.at[k], inner)

    def oc_copy(p):
        return send(OCS.at[p], OCR.at[p], oc_s, oc_r.at[p], partner)

    def ox_copy(p):
        q = lax.rem(p, 16)
        return send(OXS.at[p], OXR.at[p], ox_s, ox_r.at[p], at(lax.rem(q, 4), lax.rem(3 * q + lax.div(q, 4), 4)))

    def z_copy():
        return send(ZS, ZR, z_s, z_r, across)

    loads = [pltpu.make_async_copy(src, dst, load_sem.at[i]) for i, (src, dst) in enumerate([
        (w_in_hbm, w_in), (w_out_hbm, w_out), (act, A.at[0, 0:16]), (cot, A.at[0, 32:48]),
        (probe.at[pl.ds(pl.multiple_of(gx * 16, 16), 16)], bits)])]
    for load in loads:
        load.start()

    barrier = pltpu.get_barrier_semaphore()

    def greet(device):
        pl.semaphore_signal(barrier, inc=1, device_id=device, device_id_type=MESH)

    for q in range(1, 16):
        greet(at(q % 4, q // 4))
    greet(partner)
    greet(across)
    greet(inner)

    @pl.when(edge > 0)
    def _():
        greet(outer)

    for load in loads:
        load.wait()
    A[0, 16:32, :] = (2 * bits[...] - 1).astype(F32).astype(BF16)
    w_in_t[...] = w_in[...].T
    w_out_t[...] = w_out[...].T
    pl.semaphore_wait(barrier, 18 + lax.select(edge > 0, 1, 0))

    ac_copy(0).start()
    lax.fori_loop(1, 3, lambda p, t: (axy_copy(p).start(), t)[1], 0)
    hi_copy().start()
    lax.fori_loop(3, EARLY, lambda p, t: (axy_copy(p).start(), t)[1], 0)

    def forward(p):
        ac_copy(p).wait_recv()
        rows = pl.ds(2 * p, 2)
        PART[rows, 0:32, :] = jnp.dot(
            A[rows, 0:32, :].reshape(64, 768), w_in[...], preferred_element_type=F32).reshape(2, 32, 384)
        PART[rows, 32:48, :] = jnp.dot(
            A[rows, 32:48, :].reshape(32, 768), w_out_t[...], preferred_element_type=F32).reshape(2, 16, 384)

    def chain(k):
        @pl.when(edge == 0)
        def _():
            CS[k] = PART[k].astype(BF16)

        @pl.when(edge > 0)
        def _():
            ci_copy(k).wait_recv()
            CS[k] = (PART[k] + CI[k].astype(F32)).astype(BF16)

        @pl.when(edge < 3)
        def _():
            ci_copy(k).start()

        @pl.when(edge == 3)
        def _():
            cm_copy(k).start()

    def finish(k):
        ci_copy(k).wait_recv()
        cm_copy(k).wait_recv()
        total = PART[k] + CI[k].astype(F32) + CM[lax.div(k, 2)].astype(F32)
        hidden, tangent, upstream = total[0:16], total[16:32], total[32:48]
        dens = jnp.exp(-0.5 * hidden * hidden) * 0.3989422804014327
        cdf = 0.5 * (1.0 + lax.erf(hidden * 0.7071067811865476))
        SB[k, 0:16, :] = ((cdf + hidden * dens) * upstream).astype(BF16)
        SB[k, 16:32, :] = (dens * (2.0 - hidden * hidden) * tangent * upstream).astype(BF16)
        si_copy(k).start()
        so_copy(k).start()

    def spread(k):
        so_copy(k).wait_recv()

        @pl.when(edge > 0)
        def _():
            so_copy(k).start()

    def backward(p):
        out = jnp.dot(
            SB[pl.ds(2 * p, 2)].reshape(64, 384), w_in_t[...], preferred_element_type=F32)
        OCS[p] = out[32:64].astype(BF16)
        oc_copy(p).start()
        OP[p] = out[0:32]

    def join(p):
        oc_copy(p).wait_recv()
        total = OP[p] + OCR[p].astype(F32)

        @pl.when(lax.rem(p, 16) == 0)
        def _():
            OP[p] = total

        @pl.when(lax.rem(p, 16) != 0)
        def _():
            OXS[p] = total.astype(BF16)
            ox_copy(p).start()

    def gather_sum(own, first, last):
        def add(p, total):
            ox_copy(p).wait_recv()
            return total + OXR[p].astype(F32)

        total = OP[own]
        for lo, hi_ in first, last:
            total = lax.fori_loop(lo, hi_, add, total)
        return total

    def both(*conditions):
        return functools.reduce(jnp.logical_and, conditions)

    def pair(p):
        return both(p >= 0, p < PAIRS)

    def pass_on(p):
        @pl.when(both(p < PAIRS, p != 16))
        def _():
            @pl.when(p == FIRST)
            def _():
                hi_copy().wait_recv()
                ac_copy(16).start()

            axy_copy(p).start()

    def collected(i):
        return lax.min(lax.min(2 * i + 3, i + AHEAD + 1), PAIRS)

    def collect(p, t):
        @pl.when(p != 16)
        def _():
            axy_copy(p).wait_recv()
            ac_copy(p).start()

        return t

    def step(i, t):
        pc, pf, pb = i - LAG * edge, i - LAG * 4, i - LAG * (8 - edge)
        pj = pb - CORE_LAG
        for c in range(2):
            @pl.when(both(pair(pc), z != 3 + c))
            def _():
                chain(2 * pc + c)

            @pl.when(both(pair(pf), z == 3 + c))
            def _():
                finish(2 * pf + c)

            ps = i - LAG * (4 + lax.select(z < 3 + c, 3 + c - z, z - 3 - c))

            @pl.when(both(pair(ps), z != 3 + c))
            def _():
                spread(2 * ps + c)

            if c == 0:
                @pl.when(i < PAIRS // 2)
                def _():
                    pass_on(2 * i + EARLY)
                    pass_on(2 * i + 1 + EARLY)

                @pl.when(pair(pc))
                def _():
                    lax.fori_loop(lax.select(pc == 0, 1, collected(pc - 1)), collected(pc), collect, 0)

                    @pl.when(pc < PAIRS - 1)
                    def _():
                        forward(pc + 1)
            else:
                @pl.when(pair(pb))
                def _():
                    backward(pb)

                @pl.when(pair(pj))
                def _():
                    join(pj)

                @pl.when(pj == FIRST + 15 + HI_LAG)
                def _():
                    ZS[...] = gather_sum(16, (FIRST, 16), (17, FIRST + 16)).astype(BF16)
                    z_copy().start()

        return t

    forward(0)
    lax.fori_loop(0, PAIRS + LAG * 8 + CORE_LAG, step, 0)

    total = gather_sum(0, (1, FIRST), (FIRST + 16, PAIRS))
    z_copy().wait_recv()
    total = total + ZR[...].astype(F32)
    grad[...] = total[0:16].astype(BF16)
    curv[...] = total[16:32].astype(BF16)

    hi_copy().wait_send()
    z_copy().wait_send()

    def sent(ref, sem):
        pltpu.make_async_remote_copy(
            src_ref=ref, dst_ref=ref, send_sem=sem, recv_sem=hi_r, device_id=partner,
            device_id_type=MESH).wait_send()

    sent(A.at[0:PAIRS], ac_s)
    sent(A.at[0:PAIRS - 2], axy_s)
    sent(OCS, oc_s)
    sent(OXS.at[0:PAIRS - 2], ox_s)

    @pl.when(edge < 3)
    def _():
        sent(CS, c_s)

    @pl.when(edge == 3)
    def _():
        sent(CS.at[0:PAIRS], c_s)
        sent(SB.at[0:PAIRS], si_s)

    @pl.when(edge > 0)
    def _():
        sent(SB, so_s)


def per_device(activations, cotangent, probe, w_in, w_out):
    n, k = PAIRS, CHUNKS
    dma = pltpu.SemaphoreType.DMA
    vmem = pl.BlockSpec(memory_space=pltpu.VMEM)
    gradient, curvature = pl.pallas_call(
        kernel,
        out_shape=(jax.ShapeDtypeStruct((16, 768), BF16),) * 2,
        in_specs=[pl.BlockSpec(memory_space=pl.ANY)] * 5,
        out_specs=(vmem, vmem),
        scratch_shapes=[
            pltpu.VMEM((k, 48, 768), BF16),
            pltpu.VMEM((k, 48, 384), F32),
            pltpu.VMEM((k, 48, 384), BF16),
            pltpu.VMEM((n, 48, 384), BF16),
            pltpu.VMEM((k, 48, 384), BF16),
            pltpu.VMEM((k, 32, 384), BF16),
            pltpu.VMEM((n, 32, 768), F32),
            pltpu.VMEM((n, 32, 768), BF16),
            pltpu.VMEM((n, 32, 768), BF16),
            pltpu.VMEM((n, 32, 768), BF16),
            pltpu.VMEM((n, 32, 768), BF16),
            pltpu.VMEM((32, 768), BF16),
            pltpu.VMEM((32, 768), BF16),
            pltpu.VMEM((16, 768), jnp.int32),
            pltpu.VMEM((768, 384), BF16),
            pltpu.VMEM((384, 768), BF16),
            pltpu.VMEM((384, 768), BF16),
            pltpu.VMEM((768, 384), BF16),
            dma((5,)), dma, dma,
            dma, dma((n,)), dma, dma((n,)),
            dma, dma((k,)), dma((n,)),
            dma, dma, dma((k,)),
            dma, dma((n,)), dma, dma((n,)),
            dma, dma,
        ],
        compiler_params=pltpu.CompilerParams(
            collective_id=0, has_side_effects=True, vmem_limit_bytes=60 * 1024 * 1024),
        cost_estimate=pl.CostEstimate(flops=3_020_000_000, bytes_accessed=3_000_000, transcendentals=400_000),
    )(activations[0], cotangent[0], probe[0], w_in, w_out)
    return gradient[None], curvature[None]


def solution(mesh):
    placed = (
        P("gy", "gx", "gz"),
        P("gy", "gx", "gz"),
        P("gy", None, "gz"),
        P("gz", ("gx", "gy")),
        P(("gx", "gy"), "gz"),
    )
    return jax.shard_map(
        per_device,
        mesh=mesh,
        in_specs=placed,
        out_specs=(P("gy", "gx", "gz"), P("gy", "gx", "gz")),
        check_vma=False,
    )
```

```python
import functools

import jax
import jax.numpy as jnp
from jax import lax
from jax.experimental import pallas as pl
from jax.experimental.pallas import tpu as pltpu
from jax.sharding import PartitionSpec as P

MESH = pl.DeviceIdType.MESH
BF16, F32 = jnp.bfloat16, jnp.float32

PAIRS = 32
CHUNKS = 2 * PAIRS
FIRST = 10
FINISH = 2
TURN = 4
NEAR = 2
EARLY = 6
AHEAD = 3
CORE_LAG = 1
HI_LAG = 2


def other_half(p):
    return lax.rem(lax.div(p + 16 - FIRST, 16), 2)


def kernel(act, cot, probe, w_in_hbm, w_out_hbm, outputs,
           A, PART, CI, CM, CS, SB, OP, OCS, OCR, OXS, OXR, ZS, ZR, bits, w_in, w_out, w_in_t, w_out_t,
           load_sem, hi_s, hi_r, axy_s, axy_r, ac_s, ac_r, c_s, ci_r, cm_r, so_s, si_s, s_r,
           oc_s, oc_r, ox_s, ox_r, z_s, z_r):
    gx, gy, z = lax.axis_index("gx"), lax.axis_index("gy"), lax.axis_index("gz")
    y, core = lax.div(gx, 2), lax.rem(gx, 2)
    hi, x = lax.div(gy, 4), lax.rem(gy, 4)
    left = z < 4
    edge = lax.select(left, z, 7 - z)
    z_in = lax.select(left, z + 1, z - 1)
    z_out = lax.select(left, z - 1, z + 1)

    def at(dx, dy):
        return (lax.rem(y + dy, 4) * 2 + core, hi * 4 + lax.rem(x + dx, 4), z)

    partner = (y * 2 + 1 - core, gy, z)
    across = (gx, (1 - hi) * 4 + x, z)
    inner, outer = (gx, gy, z_in), (gx, gy, z_out)

    def send(src, dst, s, r, device):
        return pltpu.make_async_remote_copy(
            src_ref=src, dst_ref=dst, send_sem=s, recv_sem=r, device_id=device, device_id_type=MESH)

    def hi_copy():
        return send(A.at[0], A.at[32], hi_s, hi_r, across)

    def axy_copy(p):
        q = lax.rem(p, 16)
        return send(A.at[32 * other_half(p)], A.at[2 * p], axy_s, axy_r.at[p],
                    at(4 - lax.rem(q, 4), 4 - lax.rem(3 * q + lax.div(q, 4), 4)))

    def ac_copy(p):
        return send(A.at[2 * p], A.at[2 * p + 1], ac_s, ac_r.at[p], partner)

    def ci_copy(k):
        return send(CS.at[k], CI.at[k], c_s, ci_r.at[k], inner)

    def cm_copy(k):
        p = lax.div(k, 2)
        return send(CS.at[k], CM.at[p], c_s, cm_r.at[p], inner)

    def so_copy(k):
        return send(SB.at[k], SB.at[k], so_s, s_r.at[k], outer)

    def si_copy(k):
        return send(SB.at[k], SB.at[k], si_s, s_r.at[k], inner)

    def oc_copy(p):
        return send(OCS.at[p], OCR.at[p], oc_s, oc_r.at[p], partner)

    def ox_copy(p):
        q = lax.rem(p, 16)
        return send(OXS.at[p], OXR.at[p], ox_s, ox_r.at[p], at(lax.rem(q, 4), lax.rem(3 * q + lax.div(q, 4), 4)))

    def z_copy():
        return send(ZS, ZR, z_s, z_r, across)

    loads = [pltpu.make_async_copy(src, dst, load_sem.at[i]) for i, (src, dst) in enumerate([
        (w_in_hbm, w_in), (w_out_hbm, w_out), (act, A.at[0, 0:16]), (cot, A.at[0, 32:48]),
        (probe.at[pl.ds(pl.multiple_of(gx * 16, 16), 16)], bits)])]
    for load in loads:
        load.start()

    barrier = pltpu.get_barrier_semaphore()

    def greet(device):
        pl.semaphore_signal(barrier, inc=1, device_id=device, device_id_type=MESH)

    for q in range(1, 16):
        greet(at(q % 4, q // 4))
    greet(partner)
    greet(across)
    greet(inner)

    @pl.when(edge > 0)
    def _():
        greet(outer)

    for load in loads:
        load.wait()
    A[0, 16:32, :] = (2 * bits[...] - 1).astype(F32).astype(BF16)
    w_in_t[...] = w_in[...].T
    w_out_t[...] = w_out[...].T
    pl.semaphore_wait(barrier, 18 + lax.select(edge > 0, 1, 0))

    ac_copy(0).start()
    hi_copy().start()
    lax.fori_loop(1, EARLY, lambda p, t: (axy_copy(p).start(), t)[1], 0)

    def forward(p):
        ac_copy(p).wait_recv()
        rows = pl.ds(2 * p, 2)
        PART[rows, 0:32, :] = jnp.dot(
            A[rows, 0:32, :].reshape(64, 768), w_in[...], preferred_element_type=F32).reshape(2, 32, 384)
        PART[rows, 32:48, :] = jnp.dot(
            A[rows, 32:48, :].reshape(32, 768), w_out_t[...], preferred_element_type=F32).reshape(2, 16, 384)

    def chain(k):
        @pl.when(edge == 0)
        def _():
            CS[k] = PART[k].astype(BF16)

        @pl.when(edge > 0)
        def _():
            ci_copy(k).wait_recv()
            CS[k] = (PART[k] + CI[k].astype(F32)).astype(BF16)

        @pl.when(edge < 3)
        def _():
            ci_copy(k).start()

        @pl.when(edge == 3)
        def _():
            cm_copy(k).start()

    def finish(k):
        ci_copy(k).wait_recv()
        cm_copy(k).wait_recv()
        total = PART[k] + CI[k].astype(F32) + CM[lax.div(k, 2)].astype(F32)
        hidden, tangent, upstream = total[0:16], total[16:32], total[32:48]
        dens = jnp.exp(-0.5 * hidden * hidden) * 0.3989422804014327
        cdf = 0.5 * (1.0 + lax.erf(hidden * 0.7071067811865476))
        SB[k, 0:16, :] = ((cdf + hidden * dens) * upstream).astype(BF16)
        SB[k, 16:32, :] = (dens * (2.0 - hidden * hidden) * tangent * upstream).astype(BF16)
        si_copy(k).start()
        so_copy(k).start()

    def spread(k):
        so_copy(k).wait_recv()

        @pl.when(edge > 0)
        def _():
            so_copy(k).start()

    def backward(p):
        out = jnp.dot(
            SB[pl.ds(2 * p, 2)].reshape(64, 384), w_in_t[...], preferred_element_type=F32)
        OCS[p] = out[32:64].astype(BF16)
        oc_copy(p).start()
        OP[p] = out[0:32]

    def join(p):
        oc_copy(p).wait_recv()
        total = OP[p] + OCR[p].astype(F32)

        @pl.when(lax.rem(p, 16) == 0)
        def _():
            OP[p] = total

        @pl.when(lax.rem(p, 16) != 0)
        def _():
            OXS[p] = total.astype(BF16)
            ox_copy(p).start()

    def gather_sum(own, first, last):
        def add(p, total):
            ox_copy(p).wait_recv()
            return total + OXR[p].astype(F32)

        total = OP[own]
        for lo, hi_ in first, last:
            total = lax.fori_loop(lo, hi_, add, total)
        return total

    def both(*conditions):
        return functools.reduce(jnp.logical_and, conditions)

    def pair(p):
        return both(p >= 0, p < PAIRS)

    def pass_on(p):
        @pl.when(both(p < PAIRS, p != 16))
        def _():
            @pl.when(p == FIRST)
            def _():
                hi_copy().wait_recv()
                ac_copy(16).start()

            axy_copy(p).start()

    def collected(i):
        return lax.min(lax.min(2 * i + 3, i + AHEAD + 1), PAIRS)

    def collect(p, t):
        @pl.when(p != 16)
        def _():
            axy_copy(p).wait_recv()
            ac_copy(p).start()

        return t

    def step(i, t):
        pc, pf, pb = i, i - FINISH, i - TURN * (4 - edge)
        pj = pb - CORE_LAG
        for c in range(2):
            @pl.when(both(pair(pc), z != 3 + c))
            def _():
                chain(2 * pc + c)

            @pl.when(both(pair(pf), z == 3 + c))
            def _():
                finish(2 * pf + c)

            ps = pb + (lax.select(left, NEAR, 0) if c == 0 else lax.select(left, 0, NEAR))

            @pl.when(both(pair(ps), z != 3 + c))
            def _():
                spread(2 * ps + c)

            if c == 0:
                @pl.when(i < PAIRS // 2)
                def _():
                    pass_on(2 * i + EARLY)
                    pass_on(2 * i + 1 + EARLY)

                @pl.when(pair(pc))
                def _():
                    lax.fori_loop(lax.select(pc == 0, 1, collected(pc - 1)), collected(pc), collect, 0)

                    @pl.when(pc < PAIRS - 1)
                    def _():
                        forward(pc + 1)
            else:
                @pl.when(pair(pb))
                def _():
                    backward(pb)

                @pl.when(pair(pj))
                def _():
                    join(pj)

                @pl.when(pj == FIRST + 15 + HI_LAG)
                def _():
                    ZS[...] = gather_sum(16, (FIRST, 16), (17, FIRST + 16)).astype(BF16)
                    z_copy().start()

        return t

    forward(0)
    lax.fori_loop(0, PAIRS + TURN * 4 + CORE_LAG, step, 0)

    total = gather_sum(0, (1, FIRST), (FIRST + 16, PAIRS))
    z_copy().wait_recv()
    total = total + ZR[...].astype(F32)
    outputs[...] = total

    hi_copy().wait_send()
    z_copy().wait_send()

    def sent(ref, sem):
        pltpu.make_async_remote_copy(
            src_ref=ref, dst_ref=ref, send_sem=sem, recv_sem=hi_r, device_id=partner,
            device_id_type=MESH).wait_send()

    sent(A.at[0:PAIRS], ac_s)
    sent(A.at[0:PAIRS - 2], axy_s)
    sent(OCS, oc_s)
    sent(OXS.at[0:PAIRS - 2], ox_s)

    @pl.when(edge < 3)
    def _():
        sent(CS, c_s)

    @pl.when(edge == 3)
    def _():
        sent(CS.at[0:PAIRS], c_s)
        sent(SB.at[0:PAIRS], si_s)

    @pl.when(edge > 0)
    def _():
        sent(SB, so_s)


def per_device(activations, cotangent, probe, w_in, w_out):
    n, k = PAIRS, CHUNKS
    dma = pltpu.SemaphoreType.DMA
    vmem = pl.BlockSpec(memory_space=pltpu.VMEM)
    both_outputs = pl.pallas_call(
        kernel,
        out_shape=jax.ShapeDtypeStruct((32, 768), F32),
        in_specs=[pl.BlockSpec(memory_space=pl.ANY)] * 5,
        out_specs=vmem,
        scratch_shapes=[
            pltpu.VMEM((k, 48, 768), BF16),
            pltpu.VMEM((k, 48, 384), F32),
            pltpu.VMEM((k, 48, 384), BF16),
            pltpu.VMEM((n, 48, 384), BF16),
            pltpu.VMEM((k, 48, 384), BF16),
            pltpu.VMEM((k, 32, 384), BF16),
            pltpu.VMEM((n, 32, 768), F32),
            pltpu.VMEM((n, 32, 768), BF16),
            pltpu.VMEM((n, 32, 768), BF16),
            pltpu.VMEM((n, 32, 768), BF16),
            pltpu.VMEM((n, 32, 768), BF16),
            pltpu.VMEM((32, 768), BF16),
            pltpu.VMEM((32, 768), BF16),
            pltpu.VMEM((16, 768), jnp.int32),
            pltpu.VMEM((768, 384), BF16),
            pltpu.VMEM((384, 768), BF16),
            pltpu.VMEM((384, 768), BF16),
            pltpu.VMEM((768, 384), BF16),
            dma((5,)), dma, dma,
            dma, dma((n,)), dma, dma((n,)),
            dma, dma((k,)), dma((n,)),
            dma, dma, dma((k,)),
            dma, dma((n,)), dma, dma((n,)),
            dma, dma,
        ],
        compiler_params=pltpu.CompilerParams(
            collective_id=0, has_side_effects=True, vmem_limit_bytes=60 * 1024 * 1024),
        cost_estimate=pl.CostEstimate(flops=3_020_000_000, bytes_accessed=3_000_000, transcendentals=400_000),
    )(activations[0], cotangent[0], probe[0], w_in, w_out)
    return both_outputs[0:16].astype(BF16)[None], both_outputs[16:32].astype(BF16)[None]


def solution(mesh):
    placed = (
        P("gy", "gx", "gz"),
        P("gy", "gx", "gz"),
        P("gy", None, "gz"),
        P("gz", ("gx", "gy")),
        P(("gx", "gy"), "gz"),
    )
    return jax.shard_map(
        per_device,
        mesh=mesh,
        in_specs=placed,
        out_specs=(P("gy", "gx", "gz"), P("gy", "gx", "gz")),
        check_vma=False,
    )
```

```python
import functools

import jax
import jax.numpy as jnp
from jax import lax
from jax.experimental import pallas as pl
from jax.experimental.pallas import tpu as pltpu
from jax.sharding import PartitionSpec as P

MESH = pl.DeviceIdType.MESH
BF16, F32 = jnp.bfloat16, jnp.float32

PAIRS = 32
CHUNKS = 2 * PAIRS
FIRST = 10
FINISH = 3
TURN = 5
NEAR = 2
EARLY = 8
AHEAD = 2
CORE_LAG = 1
HI_LAG = 2


def other_half(p):
    return lax.rem(lax.div(p + 16 - FIRST, 16), 2)


def kernel(act, cot, probe, w_in_hbm, w_out_hbm, outputs,
           A, PART, CI, CM, CS, SB, OP, OCS, OCR, OXS, OXR, ZS, ZR, bits, w_in, w_out, w_in_t, w_out_t,
           load_sem, hi_s, hi_r, axy_s, axy_r, ac_s, ac_r, c_s, ci_r, cm_r, so_s, si_s, s_r,
           oc_s, oc_r, ox_s, ox_r, z_s, z_r):
    gx, gy, z = lax.axis_index("gx"), lax.axis_index("gy"), lax.axis_index("gz")
    y, core = lax.div(gx, 2), lax.rem(gx, 2)
    hi, x = lax.div(gy, 4), lax.rem(gy, 4)
    left = z < 4
    edge = lax.select(left, z, 7 - z)
    z_in = lax.select(left, z + 1, z - 1)
    z_out = lax.select(left, z - 1, z + 1)

    def at(dx, dy):
        return (lax.rem(y + dy, 4) * 2 + core, hi * 4 + lax.rem(x + dx, 4), z)

    partner = (y * 2 + 1 - core, gy, z)
    across = (gx, (1 - hi) * 4 + x, z)
    inner, outer = (gx, gy, z_in), (gx, gy, z_out)

    def send(src, dst, s, r, device):
        return pltpu.make_async_remote_copy(
            src_ref=src, dst_ref=dst, send_sem=s, recv_sem=r, device_id=device, device_id_type=MESH)

    def hi_copy():
        return send(A.at[0], A.at[32], hi_s, hi_r, across)

    def axy_copy(p):
        q = lax.rem(p, 16)
        return send(A.at[32 * other_half(p)], A.at[2 * p], axy_s, axy_r.at[p],
                    at(4 - lax.rem(q, 4), 4 - lax.rem(3 * q + lax.div(q, 4), 4)))

    def ac_copy(p):
        return send(A.at[2 * p], A.at[2 * p + 1], ac_s, ac_r.at[p], partner)

    def ci_copy(k):
        return send(CS.at[k], CI.at[k], c_s, ci_r.at[k], inner)

    def cm_copy(k):
        p = lax.div(k, 2)
        return send(CS.at[k], CM.at[p], c_s, cm_r.at[p], inner)

    def so_copy(k):
        return send(SB.at[k], SB.at[k], so_s, s_r.at[k], outer)

    def si_copy(k):
        return send(SB.at[k], SB.at[k], si_s, s_r.at[k], inner)

    def oc_copy(p):
        return send(OCS.at[p], OCR.at[p], oc_s, oc_r.at[p], partner)

    def ox_copy(p):
        q = lax.rem(p, 16)
        return send(OXS.at[p], OXR.at[p], ox_s, ox_r.at[p], at(lax.rem(q, 4), lax.rem(3 * q + lax.div(q, 4), 4)))

    def z_copy():
        return send(ZS, ZR, z_s, z_r, across)

    loads = [pltpu.make_async_copy(src, dst, load_sem.at[i]) for i, (src, dst) in enumerate([
        (w_in_hbm, w_in), (w_out_hbm, w_out), (act, A.at[0, 0:16]), (cot, A.at[0, 32:48]),
        (probe.at[pl.ds(pl.multiple_of(gx * 16, 16), 16)], bits)])]
    for load in loads:
        load.start()

    barrier = pltpu.get_barrier_semaphore()

    def greet(device):
        pl.semaphore_signal(barrier, inc=1, device_id=device, device_id_type=MESH)

    for q in range(1, 16):
        greet(at(q % 4, q // 4))
    greet(partner)
    greet(across)
    greet(inner)

    @pl.when(edge > 0)
    def _():
        greet(outer)

    for load in loads:
        load.wait()
    A[0, 16:32, :] = (2 * bits[...] - 1).astype(F32).astype(BF16)
    w_in_t[...] = w_in[...].T
    w_out_t[...] = w_out[...].T
    pl.semaphore_wait(barrier, 18 + lax.select(edge > 0, 1, 0))

    ac_copy(0).start()
    hi_copy().start()
    lax.fori_loop(1, EARLY, lambda p, t: (axy_copy(p).start(), t)[1], 0)

    def forward(p):
        ac_copy(p).wait_recv()
        rows = pl.ds(2 * p, 2)
        PART[rows, 0:32, :] = jnp.dot(
            A[rows, 0:32, :].reshape(64, 768), w_in[...], preferred_element_type=F32).reshape(2, 32, 384)
        PART[rows, 32:48, :] = jnp.dot(
            A[rows, 32:48, :].reshape(32, 768), w_out_t[...], preferred_element_type=F32).reshape(2, 16, 384)

    def chain(k):
        @pl.when(edge == 0)
        def _():
            CS[k] = PART[k].astype(BF16)

        @pl.when(edge > 0)
        def _():
            ci_copy(k).wait_recv()
            CS[k] = (PART[k] + CI[k].astype(F32)).astype(BF16)

        @pl.when(edge < 3)
        def _():
            ci_copy(k).start()

        @pl.when(edge == 3)
        def _():
            cm_copy(k).start()

    def finish(k):
        ci_copy(k).wait_recv()
        cm_copy(k).wait_recv()
        total = PART[k] + CI[k].astype(F32) + CM[lax.div(k, 2)].astype(F32)
        hidden, tangent, upstream = total[0:16], total[16:32], total[32:48]
        dens = jnp.exp(-0.5 * hidden * hidden) * 0.3989422804014327
        cdf = 0.5 * (1.0 + lax.erf(hidden * 0.7071067811865476))
        SB[k, 0:16, :] = ((cdf + hidden * dens) * upstream).astype(BF16)
        SB[k, 16:32, :] = (dens * (2.0 - hidden * hidden) * tangent * upstream).astype(BF16)
        si_copy(k).start()
        so_copy(k).start()

    def spread(k):
        so_copy(k).wait_recv()

        @pl.when(edge > 0)
        def _():
            so_copy(k).start()

    def backward(p):
        out = jnp.dot(
            SB[pl.ds(2 * p, 2)].reshape(64, 384), w_in_t[...], preferred_element_type=F32)
        OCS[p] = out[32:64].astype(BF16)
        oc_copy(p).start()
        OP[p] = out[0:32]

    def join(p):
        oc_copy(p).wait_recv()
        total = OP[p] + OCR[p].astype(F32)

        @pl.when(lax.rem(p, 16) == 0)
        def _():
            OP[p] = total

        @pl.when(lax.rem(p, 16) != 0)
        def _():
            OXS[p] = total.astype(BF16)
            ox_copy(p).start()

    def gather_sum(own, first, last):
        def add(p, total):
            ox_copy(p).wait_recv()
            return total + OXR[p].astype(F32)

        total = OP[own]
        for lo, hi_ in first, last:
            total = lax.fori_loop(lo, hi_, add, total)
        return total

    def both(*conditions):
        return functools.reduce(jnp.logical_and, conditions)

    def pair(p):
        return both(p >= 0, p < PAIRS)

    def pass_on(p):
        @pl.when(both(p < PAIRS, p != 16))
        def _():
            @pl.when(p == FIRST)
            def _():
                hi_copy().wait_recv()
                ac_copy(16).start()

            axy_copy(p).start()

    def collected(i):
        return lax.min(lax.min(2 * i + 3, i + AHEAD + 1), PAIRS)

    def collect(p, t):
        @pl.when(p != 16)
        def _():
            axy_copy(p).wait_recv()
            ac_copy(p).start()

        return t

    def step(i, t):
        pc, pf, pb = i, i - FINISH, i - TURN * (4 - edge)
        pj = pb - CORE_LAG
        for c in range(2):
            @pl.when(both(pair(pc), z != 3 + c))
            def _():
                chain(2 * pc + c)

        for c in range(2):
            @pl.when(both(pair(pf), z == 3 + c))
            def _():
                finish(2 * pf + c)

            ps = pb + (lax.select(left, NEAR, 0) if c == 0 else lax.select(left, 0, NEAR))

            @pl.when(both(pair(ps), z != 3 + c))
            def _():
                spread(2 * ps + c)

            if c == 0:
                @pl.when(i < PAIRS // 2)
                def _():
                    pass_on(2 * i + EARLY)
                    pass_on(2 * i + 1 + EARLY)

                @pl.when(pair(pc))
                def _():
                    lax.fori_loop(lax.select(pc == 0, 1, collected(pc - 1)), collected(pc), collect, 0)

                    @pl.when(pc < PAIRS - 1)
                    def _():
                        forward(pc + 1)
            else:
                @pl.when(pair(pb))
                def _():
                    backward(pb)

                @pl.when(pair(pj))
                def _():
                    join(pj)

                @pl.when(pj == FIRST + 15 + HI_LAG)
                def _():
                    ZS[...] = gather_sum(16, (FIRST, 16), (17, FIRST + 16)).astype(BF16)
                    z_copy().start()

        return t

    forward(0)
    lax.fori_loop(0, PAIRS + TURN * 4 + CORE_LAG, step, 0)

    total = gather_sum(0, (1, FIRST), (FIRST + 16, PAIRS))
    z_copy().wait_recv()
    total = total + ZR[...].astype(F32)
    outputs[...] = total

    hi_copy().wait_send()
    z_copy().wait_send()

    def sent(ref, sem):
        pltpu.make_async_remote_copy(
            src_ref=ref, dst_ref=ref, send_sem=sem, recv_sem=hi_r, device_id=partner,
            device_id_type=MESH).wait_send()

    sent(A.at[0:PAIRS], ac_s)
    sent(A.at[0:PAIRS - 2], axy_s)
    sent(OCS, oc_s)
    sent(OXS.at[0:PAIRS - 2], ox_s)

    @pl.when(edge < 3)
    def _():
        sent(CS, c_s)

    @pl.when(edge == 3)
    def _():
        sent(CS.at[0:PAIRS], c_s)
        sent(SB.at[0:PAIRS], si_s)

    @pl.when(edge > 0)
    def _():
        sent(SB, so_s)


def per_device(activations, cotangent, probe, w_in, w_out):
    n, k = PAIRS, CHUNKS
    dma = pltpu.SemaphoreType.DMA
    vmem = pl.BlockSpec(memory_space=pltpu.VMEM)
    both_outputs = pl.pallas_call(
        kernel,
        out_shape=jax.ShapeDtypeStruct((32, 768), F32),
        in_specs=[pl.BlockSpec(memory_space=pl.ANY)] * 5,
        out_specs=vmem,
        scratch_shapes=[
            pltpu.VMEM((k, 48, 768), BF16),
            pltpu.VMEM((k, 48, 384), F32),
            pltpu.VMEM((k, 48, 384), BF16),
            pltpu.VMEM((n, 48, 384), BF16),
            pltpu.VMEM((k, 48, 384), BF16),
            pltpu.VMEM((k, 32, 384), BF16),
            pltpu.VMEM((n, 32, 768), F32),
            pltpu.VMEM((n, 32, 768), BF16),
            pltpu.VMEM((n, 32, 768), BF16),
            pltpu.VMEM((n, 32, 768), BF16),
            pltpu.VMEM((n, 32, 768), BF16),
            pltpu.VMEM((32, 768), BF16),
            pltpu.VMEM((32, 768), BF16),
            pltpu.VMEM((16, 768), jnp.int32),
            pltpu.VMEM((768, 384), BF16),
            pltpu.VMEM((384, 768), BF16),
            pltpu.VMEM((384, 768), BF16),
            pltpu.VMEM((768, 384), BF16),
            dma((5,)), dma, dma,
            dma, dma((n,)), dma, dma((n,)),
            dma, dma((k,)), dma((n,)),
            dma, dma, dma((k,)),
            dma, dma((n,)), dma, dma((n,)),
            dma, dma,
        ],
        compiler_params=pltpu.CompilerParams(
            collective_id=0, has_side_effects=True, vmem_limit_bytes=60 * 1024 * 1024),
        cost_estimate=pl.CostEstimate(flops=3_020_000_000, bytes_accessed=3_000_000, transcendentals=400_000),
    )(activations[0], cotangent[0], probe[0], w_in, w_out)
    return both_outputs[0:16].astype(BF16)[None], both_outputs[16:32].astype(BF16)[None]


def solution(mesh):
    placed = (
        P("gy", "gx", "gz"),
        P("gy", "gx", "gz"),
        P("gy", None, "gz"),
        P("gz", ("gx", "gy")),
        P(("gx", "gy"), "gz"),
    )
    return jax.shard_map(
        per_device,
        mesh=mesh,
        in_specs=placed,
        out_specs=(P("gy", "gx", "gz"), P("gy", "gx", "gz")),
        check_vma=False,
    )
```
